32 devices in a mesh: dp: 4 (over y, x), ctx: 8 (over z, core).
Axes of the slice: x: 2, y: 2, z: 4, core: 2. Of those that a mesh axis runs over, the one named last changes fastest.
Arguments:
- query_heads: bfloat16 [8192, 16, 128], P(('dp', 'ctx')), parts along dimension 0, may hold values from -64 to 64
- key_heads: bfloat16 [8192, 8, 128], P(('dp', 'ctx')), parts along dimension 0, may hold values from -64 to 64
- value_heads: bfloat16 [8192, 8, 128], P(('dp', 'ctx')), parts along dimension 0, may hold values from -6 to 6
- grad_out: bfloat16 [8192, 16, 128], P(('dp', 'ctx')), parts along dimension 0, may hold values from -6 to 6
- doc_ids: int32 [8192], P('dp'), parts along dimension 0, may hold values from 0 to 2, as said below
Outputs:
- attended: bfloat16 [8192, 16, 128], P(('dp', 'ctx')), parts along dimension 0
- grad_query: bfloat16 [8192, 16, 128], P(('dp', 'ctx')), parts along dimension 0
- grad_key: bfloat16 [8192, 8, 128], P(('dp', 'ctx')), parts along dimension 0
- grad_value: bfloat16 [8192, 8, 128], P(('dp', 'ctx')), parts along dimension 0
The draws below stay inside these ranges and needn't reach their ends.
There are 4 independent parts, one for each index of `dp`. The reference program is written for one: setup_inputs(seed, part) draws one part's arguments, and reference() takes and returns one part's arrays. A program takes and returns all parts, laid end to end along the dimension named above; each array names one. Nothing has to cross between parts.
Inputs may be any that keep to these rules, and one draw needn't show every extreme that they name: doc_ids starts at 0 and never falls; within each aligned block of 1024 tokens it rises by one exactly once, never at the block's first token.
All inputs are finite; a program needn't handle non-finite values.
Results may differ from the reference program's by a relative error of at most 0.012.
Values may be sent and summed in bfloat16 or wider, within the bound.
A program may use at most 64 MiB of HBM per device.

```python
import jax
import jax.numpy as jnp
from jax import lax

WINDOW = 1024
HQ = 16
KVH = 8
HD = 128
TOK_DEV = 256
SEQ = 2048


def draw_query_heads(key, part):
    background = jnp.clip(jax.random.normal(jax.random.fold_in(key, 1), (SEQ, HQ, HD), jnp.float32), -4.0, 4.0)
    return jnp.clip(background, -64.0, 64.0).astype(jnp.bfloat16)


def draw_key_heads(key, part):
    background = jnp.clip(jax.random.normal(jax.random.fold_in(key, 2), (SEQ, KVH, HD), jnp.float32), -4.0, 4.0)
    return jnp.clip(background, -64.0, 64.0).astype(jnp.bfloat16)


def draw_doc_ids(key, part):
    positions = jnp.arange(SEQ)
    block_count = SEQ // WINDOW
    offsets = jax.random.randint(jax.random.fold_in(key, 3), (block_count,), 1, WINDOW)
    offsets = jnp.where(offsets % TOK_DEV == TOK_DEV // 2, offsets + 1, offsets)
    block_of = positions // WINDOW
    chosen = jnp.sum(jnp.where(block_of[:, None] == jnp.arange(block_count)[None, :], offsets[None, :], 0), axis=1)
    boundary = positions % WINDOW == chosen
    return jnp.cumsum(boundary.astype(jnp.int32)).astype(jnp.int32)


def block_levels(rng, dims, split, smallest, high):
    level = 1.0
    for position, blocks in split:
        steps = jax.random.uniform(jax.random.fold_in(jax.random.fold_in(rng, 6), position), (blocks,), jnp.float32, smallest / len(split), high / len(split))
        level = level * jnp.repeat(jnp.exp(steps), dims[position] // blocks).reshape((-1,) + (1,) * (len(dims) - 1 - position))
    return level


def centred(key, extent, width, most, split=(), kind=jnp.bfloat16):
    gain = block_levels(key, extent, split, -0.22, 0.18) if split else 1.0
    result = jax.random.normal(key, extent, jnp.float32) * width * gain
    return jnp.minimum(jnp.maximum(result, -most), most).astype(kind)


def setup_inputs(seed: int = 0, part: int = 0) -> dict:
    key_of = jax.random.split(jax.random.key(seed), 6)
    part_keys = jax.random.split(jax.random.fold_in(key_of[5], part), 6)
    query_heads = draw_query_heads(jax.random.fold_in(jax.random.fold_in(key_of[5], part), 71), part)
    key_heads = draw_key_heads(jax.random.fold_in(jax.random.fold_in(key_of[5], part), 71), part)
    value_heads = centred(part_keys[2], (SEQ, KVH, HD), 1.0, 6.0, ((0, 8),))
    grad_out = centred(part_keys[3], (SEQ, HQ, HD), 1.0, 6.0, ((0, 8),))
    doc_ids = draw_doc_ids(jax.random.fold_in(jax.random.fold_in(key_of[5], part), 71), part)
    return {"query_heads": query_heads, "key_heads": key_heads, "value_heads": value_heads, "grad_out": grad_out, "doc_ids": doc_ids}


QUERY_SCALE = 168.0 ** -0.5


def block_grads(q_blk, k_win, v_win, g_blk, q_docs, k_docs):
    row_count = q_blk.shape[0]
    col_count = k_win.shape[0]
    groups = k_win.shape[1]
    q_index = jnp.arange(row_count)[:, None]
    k_index = jnp.arange(col_count)[None, :]
    allowed = (q_docs[:, None] == k_docs[None, :]) & (k_index > q_index) & (k_index <= q_index + WINDOW)
    q_four = q_blk.astype(jnp.float32).reshape(row_count, groups, 2, -1)
    g_four = g_blk.astype(jnp.float32).reshape(row_count, groups, 2, -1)
    k_full = k_win.astype(jnp.float32)
    v_full = v_win.astype(jnp.float32)
    scores = QUERY_SCALE * jnp.einsum('rgad,cgd->garc', q_four, k_full)
    masked = jnp.where(allowed, scores, -jnp.inf)
    row_max = jnp.max(masked, axis=-1, keepdims=True)
    unnorm = jnp.exp(masked - row_max)
    weights = unnorm / jnp.sum(unnorm, axis=-1, keepdims=True)
    weights_b = weights.astype(jnp.bfloat16)
    wide_b = weights_b.astype(jnp.float32)
    attended = jnp.einsum('garc,cgd->rgad', wide_b, v_full).astype(jnp.bfloat16)
    row_dot = jnp.sum(g_four * attended.astype(jnp.float32), axis=-1)
    dprob = jnp.einsum('rgad,cgd->garc', g_four, v_full)
    dscore = (weights * (dprob - jnp.transpose(row_dot, (1, 2, 0))[..., None])).astype(jnp.bfloat16)
    dscore_f = dscore.astype(jnp.float32)
    grad_q = (QUERY_SCALE * jnp.einsum('garc,cgd->rgad', dscore_f, k_full)).astype(jnp.bfloat16)
    grad_k = (QUERY_SCALE * jnp.einsum('garc,rgad->cgd', dscore_f, q_four)).astype(jnp.bfloat16)
    grad_v = jnp.einsum('garc,rgad->cgd', wide_b, g_four).astype(jnp.bfloat16)
    return attended.reshape(q_blk.shape), grad_q.reshape(q_blk.shape), grad_k, grad_v


def reference(query_heads, key_heads, value_heads, grad_out, doc_ids):
    pieces = query_heads.shape[0] // TOK_DEV
    pad_keys = jnp.concatenate([jnp.zeros((WINDOW, KVH, HD), key_heads.dtype), key_heads], 0)
    pad_values = jnp.concatenate([jnp.zeros((WINDOW, KVH, HD), value_heads.dtype), value_heads], 0)
    pad_docs = jnp.concatenate([jnp.full((WINDOW,), -1, jnp.int32), doc_ids.astype(jnp.int32)], 0)

    def one_block(block_index):
        first_row = (block_index * TOK_DEV).astype(jnp.int32)
        q_blk = lax.dynamic_slice_in_dim(query_heads, first_row, TOK_DEV, 0)
        g_blk = lax.dynamic_slice_in_dim(grad_out, first_row, TOK_DEV, 0)
        q_docs = lax.dynamic_slice_in_dim(doc_ids.astype(jnp.int32), first_row, TOK_DEV, 0)
        k_win = lax.dynamic_slice_in_dim(pad_keys, first_row, WINDOW + TOK_DEV, 0)
        v_win = lax.dynamic_slice_in_dim(pad_values, first_row, WINDOW + TOK_DEV, 0)
        k_docs = lax.dynamic_slice_in_dim(pad_docs, first_row, WINDOW + TOK_DEV, 0)
        return block_grads(q_blk, k_win, v_win, g_blk, q_docs, k_docs)

    attended, grad_q, key_terms, value_terms = lax.map(one_block, jnp.arange(pieces, dtype=jnp.int32))

    def accumulate(block_index, totals):
        first_row = (block_index * TOK_DEV).astype(jnp.int32)
        sum_k, sum_v = totals
        part_k = lax.dynamic_slice_in_dim(sum_k, first_row, WINDOW + TOK_DEV, 0) + key_terms[block_index].astype(jnp.float32)
        part_v = lax.dynamic_slice_in_dim(sum_v, first_row, WINDOW + TOK_DEV, 0) + value_terms[block_index].astype(jnp.float32)
        sum_k = lax.dynamic_update_slice_in_dim(sum_k, part_k, first_row, 0)
        sum_v = lax.dynamic_update_slice_in_dim(sum_v, part_v, first_row, 0)
        return (sum_k, sum_v)

    empty = jnp.zeros((pieces * TOK_DEV + WINDOW, KVH, HD), jnp.float32)
    sum_k, sum_v = lax.fori_loop(0, pieces, accumulate, (empty, empty))
    seq_rows = pieces * TOK_DEV
    return (attended.reshape(seq_rows, HQ, HD), grad_q.reshape(seq_rows, HQ, HD),
            sum_k[WINDOW:].astype(jnp.bfloat16), sum_v[WINDOW:].astype(jnp.bfloat16))
```

```python
import functools

import jax
import jax.numpy as jnp
from jax import lax
from jax.experimental import pallas as pl
from jax.experimental.pallas import tpu as pltpu
from jax.sharding import PartitionSpec as P

WINDOW = 1024
QUERY_SCALE = 168.0 ** (-0.5)
F32 = jnp.float32
BF16 = jnp.bfloat16
MASKED = -1e30


def remote(src, dst, send_sem, recv_sem, ctx):
    return pltpu.make_async_remote_copy(
        src_ref=src,
        dst_ref=dst,
        send_sem=send_sem,
        recv_sem=recv_sem,
        device_id={"ctx": ctx},
        device_id_type=pl.DeviceIdType.MESH,
    )


def kernel(
    chips, half,
    q_ref, g_ref, k_ref, v_ref, qd_ref, kd_ref,
    o_ref, dq_ref, dk_ref, dv_ref,
    qs, gs, kw, vw, bias, acc, own_s, far_s, far_r, mid_s, mid_r, o_s, dq_s, fin_s,
    swap_send, swap_recv, near_send, near_recv, fwd_send, fwd_recv,
    far_send, far_recv, mid_send, mid_recv, out_send, out_recv, fin_send, fin_recv,
):
    rows = k_ref.shape[1]
    me = lax.axis_index("ctx")
    z = lax.div(me, 2)
    c = lax.rem(me, 2)
    partner = z * 2 + (1 - c)
    has_prev = z > 0
    has_prev2 = z > 1
    has_next = z < chips - 1
    mine = c * half

    barrier = pltpu.get_barrier_semaphore()

    def greet(ctx):
        pl.semaphore_signal(
            barrier, inc=1, device_id={"ctx": ctx}, device_id_type=pl.DeviceIdType.MESH
        )

    greet(partner)

    @pl.when(has_prev)
    def _():
        greet(z * 2 - 2)
        greet(z * 2 - 1)

    @pl.when(has_next)
    def _():
        greet(z * 2 + 2)
        greet(z * 2 + 3)

    links = jnp.where(has_prev, 1, 0) + jnp.where(has_next, 1, 0)
    pl.semaphore_wait(barrier, 1 + 2 * links)

    def swap_copies(hl):
        theirs = (1 - c) * half + hl
        return [
            remote(k_ref.at[theirs], kw.at[hl, 4 + c], swap_send.at[hl, 0], swap_recv.at[hl, 0], partner),
            remote(v_ref.at[theirs], vw.at[hl, 4 + c], swap_send.at[hl, 1], swap_recv.at[hl, 1], partner),
            remote(q_ref.at[theirs], qs.at[hl, c], swap_send.at[hl, 2], swap_recv.at[hl, 2], partner),
            remote(g_ref.at[theirs], gs.at[hl, c], swap_send.at[hl, 3], swap_recv.at[hl, 3], partner),
        ]

    def near_copies(hl, to):
        head = to * half + hl
        return [
            remote(k_ref.at[head], kw.at[hl, 2 + c], near_send.at[to, hl, 0], near_recv.at[c, hl, 0], z * 2 + 2 + to),
            remote(v_ref.at[head], vw.at[hl, 2 + c], near_send.at[to, hl, 1], near_recv.at[c, hl, 1], z * 2 + 2 + to),
        ]

    def near_arrivals(hl, sender):
        return [
            remote(k_ref.at[hl], kw.at[hl, 2 + sender], near_send.at[0, hl, 0], near_recv.at[sender, hl, 0], partner),
            remote(v_ref.at[hl], vw.at[hl, 2 + sender], near_send.at[0, hl, 1], near_recv.at[sender, hl, 1], partner),
        ]

    def fwd_copies(hl):
        return [
            remote(kw.at[hl, pl.ds(2, 2)], kw.at[hl, pl.ds(0, 2)], fwd_send.at[hl, 0], fwd_recv.at[hl, 0], me + 2),
            remote(vw.at[hl, pl.ds(2, 2)], vw.at[hl, pl.ds(0, 2)], fwd_send.at[hl, 1], fwd_recv.at[hl, 1], me + 2),
        ]

    def far_copy(hl):
        return remote(far_s.at[hl], far_r.at[hl], far_send.at[hl], far_recv.at[hl], me - 2)

    def mid_copy(hl):
        return remote(mid_s.at[hl], mid_r.at[hl], mid_send.at[hl], mid_recv.at[hl], me - 2)

    def out_copies(hl):
        return [
            remote(o_s.at[hl, 1 - c], o_ref.at[mine + hl], out_send.at[hl, 0], out_recv.at[hl, 0], partner),
            remote(dq_s.at[hl, 1 - c], dq_ref.at[mine + hl], out_send.at[hl, 1], out_recv.at[hl, 1], partner),
        ]

    def fin_copies(hl):
        return [
            remote(fin_s.at[hl, 0], dk_ref.at[mine + hl], fin_send.at[hl, 0], fin_recv.at[hl, 0], partner),
            remote(fin_s.at[hl, 1], dv_ref.at[mine + hl], fin_send.at[hl, 1], fin_recv.at[hl, 1], partner),
        ]

    def heads(body):
        def step(hl, carry):
            body(hl)
            return carry

        lax.fori_loop(0, half, step, 0)

    def begin(hl):
        @pl.when(has_next)
        def _():
            for to in range(2):
                for copy in near_copies(hl, to):
                    copy.start()

        for copy in swap_copies(hl):
            copy.start()

    heads(begin)

    def local(hl):
        kw[hl, 4 + c] = k_ref[mine + hl]
        vw[hl, 4 + c] = v_ref[mine + hl]
        qs[hl, c] = q_ref[mine + hl]
        gs[hl, c] = g_ref[mine + hl]

        @pl.when(z == 0)
        def _():
            kw[hl, 2:4] = jnp.zeros((2,) + kw.shape[2:], BF16)
            vw[hl, 2:4] = jnp.zeros((2,) + kw.shape[2:], BF16)

        @pl.when(z < 2)
        def _():
            kw[hl, 0:2] = jnp.zeros((2,) + kw.shape[2:], BF16)
            vw[hl, 0:2] = jnp.zeros((2,) + kw.shape[2:], BF16)

    heads(local)

    width = WINDOW + rows
    for piece in range(2):
        lower = piece * rows
        q_index = lax.broadcasted_iota(jnp.int32, (rows, width), 0)
        k_index = lax.broadcasted_iota(jnp.int32, (rows, width), 1)
        same = qd_ref[lower : lower + rows, :] == kd_ref[:, lower : lower + width]
        allowed = same & (k_index > q_index) & (k_index <= q_index + WINDOW)
        bias[piece] = jnp.where(allowed, 0.0, MASKED).astype(F32)

    blocks = width // rows

    def attend(hl, piece):
        q2 = qs[hl, piece].reshape(2 * rows, -1)
        g2 = gs[hl, piece].reshape(2 * rows, -1)
        kk = kw[hl, pl.ds(piece, blocks)].reshape(width, -1)
        vv = vw[hl, pl.ds(piece, blocks)].reshape(width, -1)
        across = (((1,), (1,)), ((), ()))
        along = (((1,), (0,)), ((), ()))
        down = (((0,), (0,)), ((), ()))
        s = lax.dot_general(q2, kk, across, preferred_element_type=F32)
        s = s.reshape(2, rows, width) + bias[piece][None]
        top = jnp.max(s, axis=-1, keepdims=True)
        p = jnp.exp((s - top) * QUERY_SCALE)
        w = (p * (1.0 / jnp.sum(p, axis=-1, keepdims=True))).reshape(2 * rows, width)
        wb = w.astype(BF16)
        o = lax.dot_general(wb, vv, along, preferred_element_type=F32).astype(BF16)
        o_s[hl, piece] = o.reshape(2, rows, -1)
        row_dot = jnp.sum(g2.astype(F32) * o.astype(F32), axis=-1, keepdims=True)
        dp = lax.dot_general(g2, vv, across, preferred_element_type=F32)
        ds = (w * (dp - row_dot)).astype(BF16)
        dq = QUERY_SCALE * lax.dot_general(ds, kk, along, preferred_element_type=F32)
        dq_s[hl, piece] = dq.astype(BF16).reshape(2, rows, -1)
        dk = QUERY_SCALE * lax.dot_general(ds, q2, down, preferred_element_type=F32)
        dv = lax.dot_general(wb, g2, down, preferred_element_type=F32)
        acc[0, pl.ds(piece, blocks)] += dk.reshape(blocks, rows, -1)
        acc[1, pl.ds(piece, blocks)] += dv.reshape(blocks, rows, -1)

    def pass_mid(hl):
        @pl.when(has_prev & has_next)
        def _():
            far_copy(hl).wait_recv()
            mid_s[hl] = (mid_s[hl].astype(F32) + far_r[hl].astype(F32)).astype(BF16)

        @pl.when(has_prev)
        def _():
            mid_copy(hl).start()

    def stage(hl):
        @pl.when(has_prev)
        def _():
            for sender in range(2):
                for copy in near_arrivals(hl, sender):
                    copy.wait_recv()

        @pl.when(has_prev & has_next)
        def _():
            for copy in fwd_copies(hl):
                copy.start()

        for copy in swap_copies(hl):
            copy.wait_recv()

        @pl.when(has_prev2)
        def _():
            for copy in fwd_copies(hl):
                copy.wait_recv()

        acc[...] = jnp.zeros_like(acc)

        def per_piece(piece, carry):
            attend(hl, piece)
            return carry

        lax.fori_loop(0, 2, per_piece, 0)
        own_s[hl] = acc[:, 4:6]
        mid_s[hl] = acc[:, 2:4].astype(BF16)
        far_s[hl] = acc[:, 0:2].astype(BF16)

        @pl.when(has_prev2)
        def _():
            far_copy(hl).start()

        for copy in out_copies(hl):
            copy.start()
        o_ref[mine + hl] = o_s[hl, c]
        dq_ref[mine + hl] = dq_s[hl, c]

        @pl.when(hl > 0)
        def _():
            pass_mid(hl - 1)

    heads(stage)
    pass_mid(half - 1)

    def finish(hl):
        @pl.when(has_next)
        def _():
            mid_copy(hl).wait_recv()
            own_s[hl] = own_s[hl] + mid_r[hl].astype(F32)

        fin_s[hl] = own_s[hl, :, 1 - c].astype(BF16)
        for copy in fin_copies(hl):
            copy.start()
        dk_ref[mine + hl] = own_s[hl, 0, c].astype(BF16)
        dv_ref[mine + hl] = own_s[hl, 1, c].astype(BF16)

    heads(finish)

    def drain(hl):
        @pl.when(has_next)
        def _():
            for to in range(2):
                for copy in near_copies(hl, to):
                    copy.wait_send()

        @pl.when(has_prev & has_next)
        def _():
            for copy in fwd_copies(hl):
                copy.wait_send()

        for copy in swap_copies(hl):
            copy.wait_send()

        @pl.when(has_prev2)
        def _():
            far_copy(hl).wait_send()

        @pl.when(has_prev)
        def _():
            mid_copy(hl).wait_send()

        for copy in out_copies(hl) + fin_copies(hl):
            copy.wait()

    heads(drain)


def body(query_heads, key_heads, value_heads, grad_out, doc_ids):
    rows, groups, size = key_heads.shape
    half = groups // 2
    count = lax.axis_size("ctx")
    chip = lax.div(lax.axis_index("ctx"), 2)
    first_row = chip * (2 * rows)
    pad_docs = jnp.concatenate([jnp.full((WINDOW,), -1, jnp.int32), doc_ids], 0)
    q_docs = lax.dynamic_slice_in_dim(doc_ids, first_row, 2 * rows, 0)[:, None]
    k_docs = lax.dynamic_slice_in_dim(pad_docs, first_row, WINDOW + 2 * rows, 0)[None, :]

    def paired(x):
        return jnp.transpose(x.reshape(rows, groups, 2, size), (1, 2, 0, 3))

    def unpaired(x):
        return jnp.transpose(x, (2, 0, 1, 3)).reshape(query_heads.shape)

    wide = jax.ShapeDtypeStruct((groups, 2, rows, size), BF16)
    slim = jax.ShapeDtypeStruct((groups, rows, size), BF16)
    slots = (WINDOW + 2 * rows) // rows
    vmem = pl.BlockSpec(memory_space=pltpu.VMEM)
    dma = pltpu.SemaphoreType.DMA
    part = (half, 2, 2, rows, size)
    attended, grad_q, grad_k, grad_v = pl.pallas_call(
        functools.partial(kernel, count // 2, half),
        out_shape=(wide, wide, slim, slim),
        in_specs=[vmem] * 6,
        out_specs=(vmem,) * 4,
        scratch_shapes=[
            pltpu.VMEM(part, BF16),
            pltpu.VMEM(part, BF16),
            pltpu.VMEM((half, slots, rows, size), BF16),
            pltpu.VMEM((half, slots, rows, size), BF16),
            pltpu.VMEM((2, rows, WINDOW + rows), F32),
            pltpu.VMEM((2, slots, rows, size), F32),
            pltpu.VMEM(part, F32),
            pltpu.VMEM(part, BF16),
            pltpu.VMEM(part, BF16),
            pltpu.VMEM(part, BF16),
            pltpu.VMEM(part, BF16),
            pltpu.VMEM(part, BF16),
            pltpu.VMEM(part, BF16),
            pltpu.VMEM((half, 2, rows, size), BF16),
            dma((half, 4)), dma((half, 4)),
            dma((2, half, 2)), dma((2, half, 2)),
            dma((half, 2)), dma((half, 2)),
            dma((half,)), dma((half,)),
            dma((half,)), dma((half,)),
            dma((half, 2)), dma((half, 2)),
            dma((half, 2)), dma((half, 2)),
        ],
        compiler_params=pltpu.CompilerParams(
            collective_id=0, has_side_effects=True, vmem_limit_bytes=60 * 1024 * 1024
        ),
    )(
        paired(query_heads), paired(grad_out),
        jnp.transpose(key_heads, (1, 0, 2)), jnp.transpose(value_heads, (1, 0, 2)),
        q_docs, k_docs,
    )
    return (
        unpaired(attended), unpaired(grad_q),
        jnp.transpose(grad_k, (1, 0, 2)), jnp.transpose(grad_v, (1, 0, 2)),
    )


def solution(mesh):
    split = P(("dp", "ctx"), None, None)
    return jax.shard_map(
        body,
        mesh=mesh,
        in_specs=(split, split, split, split, P("dp")),
        out_specs=(split, split, split, split),
        check_vma=False,
    )
```

```python
import functools

import jax
import jax.numpy as jnp
from jax import lax
from jax.experimental import pallas as pl
from jax.experimental.pallas import tpu as pltpu
from jax.sharding import PartitionSpec as P

WINDOW = 1024
QUERY_SCALE = 168.0 ** (-0.5)
F32 = jnp.float32
BF16 = jnp.bfloat16
MASKED = -1e30


def remote(src, dst, send_sem, recv_sem, ctx):
    return pltpu.make_async_remote_copy(
        src_ref=src,
        dst_ref=dst,
        send_sem=send_sem,
        recv_sem=recv_sem,
        device_id={"ctx": ctx},
        device_id_type=pl.DeviceIdType.MESH,
    )


def kernel(
    chips, half,
    q_ref, g_ref, k_ref, v_ref, qd_ref, kd_ref,
    o_ref, dq_ref, dk_ref, dv_ref,
    qs, gs, kw, vw, bias, acc, own_s, far_s, far_r, mid_s, mid_r, o_s, dq_s, fin_s,
    swap_send, swap_recv, near_send, near_recv, fwd_send, fwd_recv,
    far_send, far_recv, mid_send, mid_recv, out_send, out_recv, fin_send, fin_recv,
):
    rows = k_ref.shape[1]
    me = lax.axis_index("ctx")
    z = lax.div(me, 2)
    c = lax.rem(me, 2)
    partner = z * 2 + (1 - c)
    has_prev = z > 0
    has_prev2 = z > 1
    has_next = z < chips - 1
    mine = c * half

    barrier = pltpu.get_barrier_semaphore()

    def greet(ctx):
        pl.semaphore_signal(
            barrier, inc=1, device_id={"ctx": ctx}, device_id_type=pl.DeviceIdType.MESH
        )

    greet(partner)

    @pl.when(has_prev)
    def _():
        greet(z * 2 - 2)
        greet(z * 2 - 1)

    @pl.when(has_next)
    def _():
        greet(z * 2 + 2)
        greet(z * 2 + 3)

    links = jnp.where(has_prev, 1, 0) + jnp.where(has_next, 1, 0)
    pl.semaphore_wait(barrier, 1 + 2 * links)

    def swap_copies(hl):
        theirs = (1 - c) * half + hl
        return [
            remote(k_ref.at[theirs], kw.at[hl, 4 + c], swap_send.at[hl, 0], swap_recv.at[hl, 0], partner),
            remote(v_ref.at[theirs], vw.at[hl, 4 + c], swap_send.at[hl, 1], swap_recv.at[hl, 1], partner),
            remote(q_ref.at[theirs], qs.at[hl, c], swap_send.at[hl, 2], swap_recv.at[hl, 2], partner),
            remote(g_ref.at[theirs], gs.at[hl, c], swap_send.at[hl, 3], swap_recv.at[hl, 3], partner),
        ]

    def near_copies(hl, to):
        head = to * half + hl
        return [
            remote(k_ref.at[head], kw.at[hl, 2 + c], near_send.at[to, hl, 0], near_recv.at[c, hl, 0], z * 2 + 2 + to),
            remote(v_ref.at[head], vw.at[hl, 2 + c], near_send.at[to, hl, 1], near_recv.at[c, hl, 1], z * 2 + 2 + to),
        ]

    def near_arrivals(hl, sender):
        return [
            remote(k_ref.at[hl], kw.at[hl, 2 + sender], near_send.at[0, hl, 0], near_recv.at[sender, hl, 0], partner),
            remote(v_ref.at[hl], vw.at[hl, 2 + sender], near_send.at[0, hl, 1], near_recv.at[sender, hl, 1], partner),
        ]

    def fwd_copies(hl):
        return [
            remote(kw.at[hl, pl.ds(2, 2)], kw.at[hl, pl.ds(0, 2)], fwd_send.at[hl, 0], fwd_recv.at[hl, 0], me + 2),
            remote(vw.at[hl, pl.ds(2, 2)], vw.at[hl, pl.ds(0, 2)], fwd_send.at[hl, 1], fwd_recv.at[hl, 1], me + 2),
        ]

    def far_copy(hl):
        return remote(far_s.at[hl], far_r.at[hl], far_send.at[hl], far_recv.at[hl], me - 2)

    def mid_copy(hl):
        return remote(mid_s.at[hl], mid_r.at[hl], mid_send.at[hl], mid_recv.at[hl], me - 2)

    def out_copies(hl):
        return [
            remote(o_s.at[hl, 1 - c], o_ref.at[mine + hl], out_send.at[hl, 0], out_recv.at[hl, 0], partner),
            remote(dq_s.at[hl, 1 - c], dq_ref.at[mine + hl], out_send.at[hl, 1], out_recv.at[hl, 1], partner),
        ]

    def fin_copies(hl):
        return [
            remote(fin_s.at[hl, 0], dk_ref.at[mine + hl], fin_send.at[hl, 0], fin_recv.at[hl, 0], partner),
            remote(fin_s.at[hl, 1], dv_ref.at[mine + hl], fin_send.at[hl, 1], fin_recv.at[hl, 1], partner),
        ]

    def heads(body):
        def step(hl, carry):
            body(hl)
            return carry

        lax.fori_loop(0, half, step, 0)

    def start_near(hl):
        @pl.when(has_next)
        def _():
            for to in range(2):
                for copy in near_copies(hl, to):
                    copy.start()

    def start_fwd(hl):
        @pl.when(has_prev)
        def _():
            for sender in range(2):
                for copy in near_arrivals(hl, sender):
                    copy.wait_recv()

        @pl.when(has_prev & has_next)
        def _():
            for copy in fwd_copies(hl):
                copy.start()

    start_near(0)

    def start_swap(hl):
        for copy in swap_copies(hl):
            copy.start()

    heads(start_swap)

    def local(hl):
        kw[hl, 4 + c] = k_ref[mine + hl]
        vw[hl, 4 + c] = v_ref[mine + hl]
        qs[hl, c] = q_ref[mine + hl]
        gs[hl, c] = g_ref[mine + hl]

        @pl.when(z == 0)
        def _():
            kw[hl, 2:4] = jnp.zeros((2,) + kw.shape[2:], BF16)
            vw[hl, 2:4] = jnp.zeros((2,) + kw.shape[2:], BF16)

        @pl.when(z < 2)
        def _():
            kw[hl, 0:2] = jnp.zeros((2,) + kw.shape[2:], BF16)
            vw[hl, 0:2] = jnp.zeros((2,) + kw.shape[2:], BF16)

    heads(local)

    width = WINDOW + rows
    for piece in range(2):
        lower = piece * rows
        q_index = lax.broadcasted_iota(jnp.int32, (rows, width), 0)
        k_index = lax.broadcasted_iota(jnp.int32, (rows, width), 1)
        same = qd_ref[lower : lower + rows, :] == kd_ref[:, lower : lower + width]
        allowed = same & (k_index > q_index) & (k_index <= q_index + WINDOW)
        bias[piece] = jnp.where(allowed, 0.0, MASKED).astype(F32)

    blocks = width // rows

    def attend(hl, piece):
        q2 = qs[hl, piece].reshape(2 * rows, -1)
        g2 = gs[hl, piece].reshape(2 * rows, -1)
        kk = kw[hl, pl.ds(piece, blocks)].reshape(width, -1)
        vv = vw[hl, pl.ds(piece, blocks)].reshape(width, -1)
        across = (((1,), (1,)), ((), ()))
        along = (((1,), (0,)), ((), ()))
        down = (((0,), (0,)), ((), ()))
        s = lax.dot_general(q2, kk, across, preferred_element_type=F32)
        s = s.reshape(2, rows, width) + bias[piece][None]
        top = jnp.max(s, axis=-1, keepdims=True)
        p = jnp.exp((s - top) * QUERY_SCALE)
        w = (p * (1.0 / jnp.sum(p, axis=-1, keepdims=True))).reshape(2 * rows, width)
        wb = w.astype(BF16)
        o = lax.dot_general(wb, vv, along, preferred_element_type=F32).astype(BF16)
        o_s[hl, piece] = o.reshape(2, rows, -1)
        row_dot = jnp.sum(g2.astype(F32) * o.astype(F32), axis=-1, keepdims=True)
        dp = lax.dot_general(g2, vv, across, preferred_element_type=F32)
        ds = (w * (dp - row_dot)).astype(BF16)
        dq = QUERY_SCALE * lax.dot_general(ds, kk, along, preferred_element_type=F32)
        dq_s[hl, piece] = dq.astype(BF16).reshape(2, rows, -1)
        dk = QUERY_SCALE * lax.dot_general(ds, q2, down, preferred_element_type=F32)
        dv = lax.dot_general(wb, g2, down, preferred_element_type=F32)
        acc[0, pl.ds(piece, blocks)] += dk.reshape(blocks, rows, -1)
        acc[1, pl.ds(piece, blocks)] += dv.reshape(blocks, rows, -1)

    def pass_mid(hl):
        @pl.when(has_prev & has_next)
        def _():
            far_copy(hl).wait_recv()
            mid_s[hl] = (mid_s[hl].astype(F32) + far_r[hl].astype(F32)).astype(BF16)

        @pl.when(has_prev)
        def _():
            mid_copy(hl).start()

    def stage(hl):
        for copy in swap_copies(hl):
            copy.wait_recv()

        @pl.when(has_prev2)
        def _():
            for copy in fwd_copies(hl):
                copy.wait_recv()

        @pl.when(hl + 1 < half)
        def _():
            start_near(hl + 1)

        acc[...] = jnp.zeros_like(acc)

        def per_piece(piece, carry):
            attend(hl, piece)

            @pl.when((hl + 1 < half) & (piece == 0))
            def _():
                start_fwd(hl + 1)

            return carry

        lax.fori_loop(0, 2, per_piece, 0)
        own_s[hl] = acc[:, 4:6]
        mid_s[hl] = acc[:, 2:4].astype(BF16)
        far_s[hl] = acc[:, 0:2].astype(BF16)

        @pl.when(has_prev2)
        def _():
            far_copy(hl).start()

        for copy in out_copies(hl):
            copy.start()
        o_ref[mine + hl] = o_s[hl, c]
        dq_ref[mine + hl] = dq_s[hl, c]

        @pl.when(hl > 0)
        def _():
            pass_mid(hl - 1)

    start_fwd(0)
    heads(stage)
    pass_mid(half - 1)

    def finish(hl):
        @pl.when(has_next)
        def _():
            mid_copy(hl).wait_recv()
            own_s[hl] = own_s[hl] + mid_r[hl].astype(F32)

        fin_s[hl] = own_s[hl, :, 1 - c].astype(BF16)
        for copy in fin_copies(hl):
            copy.start()
        dk_ref[mine + hl] = own_s[hl, 0, c].astype(BF16)
        dv_ref[mine + hl] = own_s[hl, 1, c].astype(BF16)

    heads(finish)

    def drain(hl):
        @pl.when(has_next)
        def _():
            for to in range(2):
                for copy in near_copies(hl, to):
                    copy.wait_send()

        @pl.when(has_prev & has_next)
        def _():
            for copy in fwd_copies(hl):
                copy.wait_send()

        for copy in swap_copies(hl):
            copy.wait_send()

        @pl.when(has_prev2)
        def _():
            far_copy(hl).wait_send()

        @pl.when(has_prev)
        def _():
            mid_copy(hl).wait_send()

        for copy in out_copies(hl) + fin_copies(hl):
            copy.wait()

    heads(drain)


def body(query_heads, key_heads, value_heads, grad_out, doc_ids):
    rows, groups, size = key_heads.shape
    half = groups // 2
    count = lax.axis_size("ctx")
    chip = lax.div(lax.axis_index("ctx"), 2)
    first_row = chip * (2 * rows)
    pad_docs = jnp.concatenate([jnp.full((WINDOW,), -1, jnp.int32), doc_ids], 0)
    q_docs = lax.dynamic_slice_in_dim(doc_ids, first_row, 2 * rows, 0)[:, None]
    k_docs = lax.dynamic_slice_in_dim(pad_docs, first_row, WINDOW + 2 * rows, 0)[None, :]

    def paired(x):
        return jnp.transpose(x.reshape(rows, groups, 2, size), (1, 2, 0, 3))

    def unpaired(x):
        return jnp.transpose(x, (2, 0, 1, 3)).reshape(query_heads.shape)

    wide = jax.ShapeDtypeStruct((groups, 2, rows, size), BF16)
    slim = jax.ShapeDtypeStruct((groups, rows, size), BF16)
    slots = (WINDOW + 2 * rows) // rows
    vmem = pl.BlockSpec(memory_space=pltpu.VMEM)
    dma = pltpu.SemaphoreType.DMA
    part = (half, 2, 2, rows, size)
    attended, grad_q, grad_k, grad_v = pl.pallas_call(
        functools.partial(kernel, count // 2, half),
        out_shape=(wide, wide, slim, slim),
        in_specs=[vmem] * 6,
        out_specs=(vmem,) * 4,
        scratch_shapes=[
            pltpu.VMEM(part, BF16),
            pltpu.VMEM(part, BF16),
            pltpu.VMEM((half, slots, rows, size), BF16),
            pltpu.VMEM((half, slots, rows, size), BF16),
            pltpu.VMEM((2, rows, WINDOW + rows), F32),
            pltpu.VMEM((2, slots, rows, size), F32),
            pltpu.VMEM(part, F32),
            pltpu.VMEM(part, BF16),
            pltpu.VMEM(part, BF16),
            pltpu.VMEM(part, BF16),
            pltpu.VMEM(part, BF16),
            pltpu.VMEM(part, BF16),
            pltpu.VMEM(part, BF16),
            pltpu.VMEM((half, 2, rows, size), BF16),
            dma((half, 4)), dma((half, 4)),
            dma((2, half, 2)), dma((2, half, 2)),
            dma((half, 2)), dma((half, 2)),
            dma((half,)), dma((half,)),
            dma((half,)), dma((half,)),
            dma((half, 2)), dma((half, 2)),
            dma((half, 2)), dma((half, 2)),
        ],
        compiler_params=pltpu.CompilerParams(
            collective_id=0, has_side_effects=True, vmem_limit_bytes=60 * 1024 * 1024
        ),
    )(
        paired(query_heads), paired(grad_out),
        jnp.transpose(key_heads, (1, 0, 2)), jnp.transpose(value_heads, (1, 0, 2)),
        q_docs, k_docs,
    )
    return (
        unpaired(attended), unpaired(grad_q),
        jnp.transpose(grad_k, (1, 0, 2)), jnp.transpose(grad_v, (1, 0, 2)),
    )


def solution(mesh):
    split = P(("dp", "ctx"), None, None)
    return jax.shard_map(
        body,
        mesh=mesh,
        in_specs=(split, split, split, split, P("dp")),
        out_specs=(split, split, split, split),
        check_vma=False,
    )
```

```python
import functools

import jax
import jax.numpy as jnp
from jax import lax
from jax.experimental import pallas as pl
from jax.experimental.pallas import tpu as pltpu
from jax.sharding import PartitionSpec as P

WINDOW = 1024
QUERY_SCALE = 168.0 ** (-0.5)
F32 = jnp.float32
BF16 = jnp.bfloat16
MASKED = -1e30


def remote(src, dst, send_sem, recv_sem, ctx):
    return pltpu.make_async_remote_copy(
        src_ref=src,
        dst_ref=dst,
        send_sem=send_sem,
        recv_sem=recv_sem,
        device_id={"ctx": ctx},
        device_id_type=pl.DeviceIdType.MESH,
    )


def kernel(
    chips, half,
    q_in, g_in, k_ref, v_ref, docs_ref,
    o_ref, dq_ref, dk_ref, dv_ref,
    tall, q_ref, g_ref, qs, gs, kw, vw, bias, acc, own_s, far_s, far_r, mid_s, mid_r, o_s, dq_s, fin_s,
    swap_send, swap_recv, near_send, near_recv, fwd_send, fwd_recv,
    far_send, far_recv, mid_send, mid_recv, out_send, out_recv, fin_send, fin_recv,
):
    rows = k_ref.shape[1]
    me = lax.axis_index("ctx")
    z = lax.div(me, 2)
    c = lax.rem(me, 2)
    partner = z * 2 + (1 - c)
    has_prev = z > 0
    has_prev2 = z > 1
    has_next = z < chips - 1
    mine = c * half

    barrier = pltpu.get_barrier_semaphore()

    def greet(ctx):
        pl.semaphore_signal(
            barrier, inc=1, device_id={"ctx": ctx}, device_id_type=pl.DeviceIdType.MESH
        )

    greet(partner)

    @pl.when(has_prev)
    def _():
        greet(z * 2 - 2)
        greet(z * 2 - 1)

    @pl.when(has_next)
    def _():
        greet(z * 2 + 2)
        greet(z * 2 + 3)

    links = jnp.where(has_prev, 1, 0) + jnp.where(has_next, 1, 0)
    pl.semaphore_wait(barrier, 1 + 2 * links)

    def swap_copies(hl):
        theirs = (1 - c) * half + hl
        return [
            remote(k_ref.at[theirs], kw.at[hl, 4 + c], swap_send.at[hl, 0], swap_recv.at[hl, 0], partner),
            remote(v_ref.at[theirs], vw.at[hl, 4 + c], swap_send.at[hl, 1], swap_recv.at[hl, 1], partner),
            remote(q_ref.at[theirs], qs.at[hl, c], swap_send.at[hl, 2], swap_recv.at[hl, 2], partner),
            remote(g_ref.at[theirs], gs.at[hl, c], swap_send.at[hl, 3], swap_recv.at[hl, 3], partner),
        ]

    def near_copies(hl, to):
        head = to * half + hl
        return [
            remote(k_ref.at[head], kw.at[hl, 2 + c], near_send.at[to, hl, 0], near_recv.at[c, hl, 0], z * 2 + 2 + to),
            remote(v_ref.at[head], vw.at[hl, 2 + c], near_send.at[to, hl, 1], near_recv.at[c, hl, 1], z * 2 + 2 + to),
        ]

    def near_arrivals(hl, sender):
        return [
            remote(k_ref.at[hl], kw.at[hl, 2 + sender], near_send.at[0, hl, 0], near_recv.at[sender, hl, 0], partner),
            remote(v_ref.at[hl], vw.at[hl, 2 + sender], near_send.at[0, hl, 1], near_recv.at[sender, hl, 1], partner),
        ]

    def fwd_copies(hl):
        return [
            remote(kw.at[hl, pl.ds(2, 2)], kw.at[hl, pl.ds(0, 2)], fwd_send.at[hl, 0], fwd_recv.at[hl, 0], me + 2),
            remote(vw.at[hl, pl.ds(2, 2)], vw.at[hl, pl.ds(0, 2)], fwd_send.at[hl, 1], fwd_recv.at[hl, 1], me + 2),
        ]

    def far_copy(hl):
        return remote(far_s.at[hl], far_r.at[hl], far_send.at[hl], far_recv.at[hl], me - 2)

    def mid_copy(hl):
        return remote(mid_s.at[hl], mid_r.at[hl], mid_send.at[hl], mid_recv.at[hl], me - 2)

    def out_copies(hl):
        return [
            remote(o_s.at[hl, 1 - c], o_ref.at[mine + hl], out_send.at[hl, 0], out_recv.at[hl, 0], partner),
            remote(dq_s.at[hl, 1 - c], dq_ref.at[mine + hl], out_send.at[hl, 1], out_recv.at[hl, 1], partner),
        ]

    def fin_copies(hl):
        return [
            remote(fin_s.at[hl, 0], dk_ref.at[mine + hl], fin_send.at[hl, 0], fin_recv.at[hl, 0], partner),
            remote(fin_s.at[hl, 1], dv_ref.at[mine + hl], fin_send.at[hl, 1], fin_recv.at[hl, 1], partner),
        ]

    def heads(body):
        def step(hl, carry):
            body(hl)
            return carry

        lax.fori_loop(0, half, step, 0)

    def start_near(hl):
        @pl.when(has_next)
        def _():
            for to in range(2):
                for copy in near_copies(hl, to):
                    copy.start()

    def start_fwd(hl):
        @pl.when(has_prev)
        def _():
            for sender in range(2):
                for copy in near_arrivals(hl, sender):
                    copy.wait_recv()

        @pl.when(has_prev & has_next)
        def _():
            for copy in fwd_copies(hl):
                copy.start()

    start_near(0)

    for whole, split in ((q_in, q_ref), (g_in, g_ref)):
        tall[...] = whole[...].astype(F32)
        for head in range(2 * split.shape[0]):
            split[head // 2, head % 2] = tall[:, head, :].astype(BF16)

    def start_swap(hl):
        for copy in swap_copies(hl):
            copy.start()

    heads(start_swap)

    def local(hl):
        kw[hl, 4 + c] = k_ref[mine + hl]
        vw[hl, 4 + c] = v_ref[mine + hl]
        qs[hl, c] = q_ref[mine + hl]
        gs[hl, c] = g_ref[mine + hl]

        @pl.when(z == 0)
        def _():
            kw[hl, 2:4] = jnp.zeros((2,) + kw.shape[2:], BF16)
            vw[hl, 2:4] = jnp.zeros((2,) + kw.shape[2:], BF16)

        @pl.when(z < 2)
        def _():
            kw[hl, 0:2] = jnp.zeros((2,) + kw.shape[2:], BF16)
            vw[hl, 0:2] = jnp.zeros((2,) + kw.shape[2:], BF16)

    heads(local)

    width = WINDOW + rows
    for piece in range(2):
        lower = piece * rows
        q_index = lax.broadcasted_iota(jnp.int32, (rows, width), 0)
        k_index = lax.broadcasted_iota(jnp.int32, (rows, width), 1)
        first = pl.multiple_of(z * (2 * rows) + lower, rows)
        k_docs = docs_ref[:, pl.ds(first, width)].astype(F32)
        q_docs = docs_ref[:, pl.ds(first + WINDOW, rows)].astype(F32)
        q_docs = jnp.transpose(jnp.broadcast_to(q_docs, (rows, rows)))[:, :1]
        same = q_docs == k_docs
        allowed = same & (k_index > q_index) & (k_index <= q_index + WINDOW)
        bias[piece] = jnp.where(allowed, 0.0, MASKED).astype(F32)

    blocks = width // rows

    def attend(hl, piece):
        q2 = qs[hl, piece].reshape(2 * rows, -1)
        g2 = gs[hl, piece].reshape(2 * rows, -1)
        kk = kw[hl, pl.ds(piece, blocks)].reshape(width, -1)
        vv = vw[hl, pl.ds(piece, blocks)].reshape(width, -1)
        across = (((1,), (1,)), ((), ()))
        along = (((1,), (0,)), ((), ()))
        down = (((0,), (0,)), ((), ()))
        s = lax.dot_general(q2, kk, across, preferred_element_type=F32)
        s = s.reshape(2, rows, width) + bias[piece][None]
        top = jnp.max(s, axis=-1, keepdims=True)
        p = jnp.exp((s - top) * QUERY_SCALE)
        w = (p * (1.0 / jnp.sum(p, axis=-1, keepdims=True))).reshape(2 * rows, width)
        wb = w.astype(BF16)
        o = lax.dot_general(wb, vv, along, preferred_element_type=F32).astype(BF16)
        o_s[hl, piece] = o.reshape(2, rows, -1)
        row_dot = jnp.sum(g2.astype(F32) * o.astype(F32), axis=-1, keepdims=True)
        dp = lax.dot_general(g2, vv, across, preferred_element_type=F32)
        ds = (w * (dp - row_dot)).astype(BF16)
        dq = QUERY_SCALE * lax.dot_general(ds, kk, along, preferred_element_type=F32)
        dq_s[hl, piece] = dq.astype(BF16).reshape(2, rows, -1)
        dk = QUERY_SCALE * lax.dot_general(ds, q2, down, preferred_element_type=F32)
        dv = lax.dot_general(wb, g2, down, preferred_element_type=F32)
        acc[0, pl.ds(piece, blocks)] += dk.reshape(blocks, rows, -1)
        acc[1, pl.ds(piece, blocks)] += dv.reshape(blocks, rows, -1)

    def pass_mid(hl):
        @pl.when(has_prev & has_next)
        def _():
            far_copy(hl).wait_recv()
            mid_s[hl] = (mid_s[hl].astype(F32) + far_r[hl].astype(F32)).astype(BF16)

        @pl.when(has_prev)
        def _():
            mid_copy(hl).start()

    def stage(hl):
        for copy in swap_copies(hl):
            copy.wait_recv()

        @pl.when(has_prev2)
        def _():
            for copy in fwd_copies(hl):
                copy.wait_recv()

        @pl.when(hl + 1 < half)
        def _():
            start_near(hl + 1)

        acc[...] = jnp.zeros_like(acc)

        def per_piece(piece, carry):
            attend(hl, piece)

            @pl.when((hl + 1 < half) & (piece == 0))
            def _():
                start_fwd(hl + 1)

            return carry

        lax.fori_loop(0, 2, per_piece, 0)
        own_s[hl] = acc[:, 4:6]
        mid_s[hl] = acc[:, 2:4].astype(BF16)
        far_s[hl] = acc[:, 0:2].astype(BF16)

        @pl.when(has_prev2)
        def _():
            far_copy(hl).start()

        for copy in out_copies(hl):
            copy.start()
        o_ref[mine + hl] = o_s[hl, c]
        dq_ref[mine + hl] = dq_s[hl, c]

        @pl.when(hl > 0)
        def _():
            pass_mid(hl - 1)

    start_fwd(0)
    heads(stage)
    pass_mid(half - 1)

    def finish(hl):
        @pl.when(has_next)
        def _():
            mid_copy(hl).wait_recv()
            own_s[hl] = own_s[hl] + mid_r[hl].astype(F32)

        fin_s[hl] = own_s[hl, :, 1 - c].astype(BF16)
        for copy in fin_copies(hl):
            copy.start()
        dk_ref[mine + hl] = own_s[hl, 0, c].astype(BF16)
        dv_ref[mine + hl] = own_s[hl, 1, c].astype(BF16)

    heads(finish)

    def drain(hl):
        @pl.when(has_next)
        def _():
            for to in range(2):
                for copy in near_copies(hl, to):
                    copy.wait_send()

        @pl.when(has_prev & has_next)
        def _():
            for copy in fwd_copies(hl):
                copy.wait_send()

        for copy in swap_copies(hl):
            copy.wait_send()

        @pl.when(has_prev2)
        def _():
            far_copy(hl).wait_send()

        @pl.when(has_prev)
        def _():
            mid_copy(hl).wait_send()

        for copy in out_copies(hl) + fin_copies(hl):
            copy.wait()

    heads(drain)


def body(query_heads, key_heads, value_heads, grad_out, doc_ids):
    rows, groups, size = key_heads.shape
    half = groups // 2
    count = lax.axis_size("ctx")
    pad_docs = jnp.concatenate([jnp.full((WINDOW,), -1, jnp.int32), doc_ids], 0)[None, :]

    def unpaired(x):
        return jnp.transpose(x, (2, 0, 1, 3)).reshape(query_heads.shape)

    wide = jax.ShapeDtypeStruct((groups, 2, rows, size), BF16)
    slim = jax.ShapeDtypeStruct((groups, rows, size), BF16)
    slots = (WINDOW + 2 * rows) // rows
    vmem = pl.BlockSpec(memory_space=pltpu.VMEM)
    dma = pltpu.SemaphoreType.DMA
    part = (half, 2, 2, rows, size)
    attended, grad_q, grad_k, grad_v = pl.pallas_call(
        functools.partial(kernel, count // 2, half),
        out_shape=(wide, wide, slim, slim),
        in_specs=[vmem] * 5,
        out_specs=(vmem,) * 4,
        scratch_shapes=[
            pltpu.VMEM(query_heads.shape, F32),
            pltpu.VMEM((groups, 2, rows, size), BF16),
            pltpu.VMEM((groups, 2, rows, size), BF16),
            pltpu.VMEM(part, BF16),
            pltpu.VMEM(part, BF16),
            pltpu.VMEM((half, slots, rows, size), BF16),
            pltpu.VMEM((half, slots, rows, size), BF16),
            pltpu.VMEM((2, rows, WINDOW + rows), F32),
            pltpu.VMEM((2, slots, rows, size), F32),
            pltpu.VMEM(part, F32),
            pltpu.VMEM(part, BF16),
            pltpu.VMEM(part, BF16),
            pltpu.VMEM(part, BF16),
            pltpu.VMEM(part, BF16),
            pltpu.VMEM(part, BF16),
            pltpu.VMEM(part, BF16),
            pltpu.VMEM((half, 2, rows, size), BF16),
            dma((half, 4)), dma((half, 4)),
            dma((2, half, 2)), dma((2, half, 2)),
            dma((half, 2)), dma((half, 2)),
            dma((half,)), dma((half,)),
            dma((half,)), dma((half,)),
            dma((half, 2)), dma((half, 2)),
            dma((half, 2)), dma((half, 2)),
        ],
        compiler_params=pltpu.CompilerParams(
            collective_id=0, has_side_effects=True, vmem_limit_bytes=60 * 1024 * 1024
        ),
    )(
        query_heads, grad_out,
        jnp.transpose(key_heads, (1, 0, 2)), jnp.transpose(value_heads, (1, 0, 2)),
        pad_docs,
    )
    return (
        unpaired(attended), unpaired(grad_q),
        jnp.transpose(grad_k, (1, 0, 2)), jnp.transpose(grad_v, (1, 0, 2)),
    )


def solution(mesh):
    split = P(("dp", "ctx"), None, None)
    return jax.shard_map(
        body,
        mesh=mesh,
        in_specs=(split, split, split, split, P("dp")),
        out_specs=(split, split, split, split),
        check_vma=False,
    )
```
